32 devices in a mesh: grp: 2 (over x), ep: 8 (over z, y), tp: 2 (over core).
Axes of the slice: x: 2, y: 2, z: 4, core: 2. Of those that a mesh axis runs over, the one named last changes fastest.
Arguments:
- query_rows: bfloat16 [1024, 1152], P(('grp', 'ep'), 'tp'), parts along dimension 0, may hold values from -160 to 160, as said below
- key_rows: bfloat16 [1024, 1152], P(('grp', 'ep'), 'tp'), parts along dimension 0, may hold values from -4 to 4
- value_rows: bfloat16 [1024, 1152], P(('grp', 'ep'), 'tp'), parts along dimension 0, may hold values from -6 to 6
- merger_weight: bfloat16 [4, 1152, 4096], P(None, 'tp', 'ep'), may hold values from -0.09375 to 0.09375
- visual_counts: int32 [16], P('grp'), parts along dimension 0, may hold values from 1 to 32, 128 in all
- text_rows: bfloat16 [512, 4096], P(('grp', 'ep')), parts along dimension 0, may hold values from -6 to 6
- norm_gain: float32 [4096], replicated, may hold values from 0.1 to 1.9
- route_ids: int32 [1024, 8], P(('grp', 'ep')), parts along dimension 0, may hold values from 0 to 31, all different within a row; in each aligned block of 32 rows (0 to 31, 32 to 63, ...) at most 16 rows name the same one
- route_gates: float32 [1024, 8], P(('grp', 'ep')), parts along dimension 0, may hold values from 0.03 to 0.4
- gate_weight: bfloat16 [32, 4096, 768], P('ep', None, 'tp'), may hold values from -0.09375 to 0.09375
- up_weight: bfloat16 [32, 4096, 768], P('ep', None, 'tp'), may hold values from -0.09375 to 0.09375
- down_weight: bfloat16 [32, 768, 4096], P('ep', 'tp'), may hold values from -0.21875 to 0.21875
Outputs:
- moe_out: bfloat16 [1024, 4096], P(('grp', 'ep')), parts along dimension 0
The draws below stay inside these ranges and needn't reach their ends.
There are 2 independent parts, one for each index of `grp`. The reference program is written for one: setup_inputs(seed, part) draws one part's arguments, and reference() takes and returns one part's arrays. A program takes and returns all parts, laid end to end along the dimension named above; an argument that names none is the same for every part. Nothing has to cross between parts.
Inputs may be any that keep to these rules, and one draw needn't show every extreme that they name: `query_rows`: rows of the image in order. `visual_counts`: visual rows for each language owner in order of owners; they sum to 128 and the largest is exactly 32. `route_ids`: each row names 8 different experts; in each aligned block of 32 rows no expert is named by more than 16 rows; ids of visual slots at or past their owner's count are not used.
All inputs are finite; a program needn't handle non-finite values.
Results may differ from the reference program's by a relative error of at most 0.0065.
Values may be sent and summed in bfloat16 or wider, within the bound.
A program may use at most 128 MiB of HBM per device.

```python
import math
import jax
import jax.numpy as jnp
import numpy as np
from jax import lax

VDIM = 1152
HEADS = 16
HEAD_DIM = 72
MERGE = 4
D = 4096
FF = 768
EXPERTS = 32
TOP = 8
LANG_DEV = 32
PATCHES = 512
VIS = 128
VCAP = 32
SHARE = 32
CAPACITY = 16
TEXT = 256
ROWS = 512
N_EP = 8
N_TP = 2


def attention_pair(key, spike_share):
    base_key = jax.random.fold_in(key, 0)
    pick_key = jax.random.fold_in(key, 1)
    row_key = jax.random.fold_in(key, 3)
    noise_key = jax.random.fold_in(key, 4)
    keys_base = jax.random.truncated_normal(base_key, -4.0, 4.0, (PATCHES, VDIM), jnp.float32)
    chosen = (jax.random.randint(pick_key, (PATCHES,), 0, 32) == 0).astype(jnp.float32) * spike_share
    partner = 2 * jax.random.randint(row_key, (PATCHES,), 0, PATCHES // 2)
    flagged = jnp.zeros((PATCHES // 2,), jnp.float32).at[partner // 2].max(chosen)
    paired = keys_base.reshape(PATCHES // 2, 2, VDIM)
    even_rows = paired[:, 0, :]
    odd_rows = paired[:, 1, :] + flagged[:, None] * (0.99 * paired[:, 0, :] - paired[:, 1, :])
    keys_out = jnp.stack([even_rows, odd_rows], axis=1).reshape(PATCHES, VDIM)
    drawn = 2.5 * jax.random.truncated_normal(noise_key, -4.0, 4.0, (PATCHES, VDIM), jnp.float32)
    queries_out = drawn
    return (queries_out, keys_out)


def draw_query_rows(key, part):
    spike_share = 0.0
    queries_out, keys_out = attention_pair(key, spike_share)
    return queries_out.astype(jnp.bfloat16)


def draw_key_rows(key, part):
    spike_share = 0.0
    queries_out, keys_out = attention_pair(key, spike_share)
    return keys_out.astype(jnp.bfloat16)


def levels(rng, shape, cuts, low, high):
    loudness, own = 1.0, jax.random.fold_in(rng, 6)
    for position, shards_of in cuts:
        steps = jnp.exp(jax.random.uniform(jax.random.fold_in(own, position), (shards_of,), jnp.float32, low / len(cuts), high / len(cuts)))
        loudness = loudness * jnp.repeat(steps, shape[position] // shards_of).reshape([-1 if axis == position else 1 for axis in range(len(shape))])
    return loudness


def split_up(number_of, total, limit, skew):
    loads = [(1 << 20) // math.isqrt(standing ** skew) + 1 for standing in range(2, number_of + 1)]
    rest, holding = total - limit - (number_of - 1), [1] * (number_of - 1)
    while rest > 0:
        candidates = [i for i in range(number_of - 1) if holding[i] < limit]
        pool, budget = sum([loads[i] for i in candidates]), rest
        for i in candidates:
            extra = min(limit - holding[i], max(1, budget * loads[i] // pool), rest)
            holding[i] = holding[i] + extra
            rest = rest - extra
    return np.array([limit] + holding)


def ragged_sizes(rng, amount, total, most, slope):
    if amount == 2:
        one = jax.random.randint(rng, (), max(1, total - most), min(most, total - 1) + 1)
        return jnp.stack([one, total - one])
    sizes = jnp.asarray(split_up(amount, total, most, slope), jnp.int32)
    couples = (amount - 1) // 2
    donor, taker = sizes[1:1 + 2 * couples:2], sizes[2:2 + 2 * couples:2]
    slack = jnp.minimum(donor - 1, most - taker)
    passed = jax.random.randint(jax.random.fold_in(rng, 1), (couples,), 0, 1 << 20) % (slack + 1)
    sizes = sizes.at[1:1 + 2 * couples:2].set(donor - passed).at[2:2 + 2 * couples:2].set(taker + passed)
    return sizes[jax.random.permutation(jax.random.fold_in(rng, 2), amount)]


def shared_out(own_key, own, number, rows, count, top, reach, slope):
    sequence = jax.random.permutation(own_key, count)
    packed, ordinary = load_shares(count, rows * top, reach, slope, True), load_shares(count, rows * top, reach, slope, False)
    places = jnp.arange(count)

    def named(lengths, turn):
        used = int((lengths > 0).sum())
        fixed = max(1, used // 4)
        moved = fixed + (places - fixed + turn * (used - fixed)) % max(1, count - fixed)
        return jnp.zeros((count,), jnp.int32).at[sequence[jnp.where(places < fixed, places, moved)]].set(jnp.asarray(lengths, jnp.int32))

    lengths = jnp.where(number % 4 == 0, named(packed, number // 4), named(ordinary, number - number // 4 - 1))
    mixed = jax.random.permutation(jax.random.fold_in(own, 3), count)
    giver, sink = mixed[0:count // 2 * 2:2], mixed[1:count // 2 * 2:2]
    room = jnp.minimum(lengths[giver] - 1, reach - lengths[sink]) // 2
    room = jnp.where((giver == sequence[0]) | (sink == sequence[0]) | (lengths[sink] == 0), 0, jnp.maximum(room, 0))
    moved = jax.random.randint(jax.random.fold_in(own, 4), (count // 2,), 0, 1 << 20) % (room + 1)
    lengths = lengths.at[giver].add(-moved).at[sink].add(moved)
    items = jnp.searchsorted(jnp.cumsum(lengths), jnp.arange(rows * top), side="right").astype(jnp.int32)
    table = items.reshape(top, rows).T
    table = table[jax.random.permutation(jax.random.fold_in(own, 1), rows)]
    turn = jax.random.randint(jax.random.fold_in(own, 2), (rows, 1), 0, top)
    return jnp.take_along_axis(table, (jnp.arange(top)[None, :] + turn) % top, axis=1)


def load_shares(amount, total, limit, lean, full):
    weights = [(1 << 20) // math.isqrt(grade ** lean) + 1 for grade in range(1, amount + 1)]
    largest = limit if full else min(limit, max(-(-total // amount), total * weights[0] // sum(weights)))
    least = 1 if total - largest >= amount - 1 else 0
    holding, surplus = [largest] + [least] * (amount - 1), total - largest - least * (amount - 1)
    while surplus > 0:
        candidates = [i for i in range(1, amount) if holding[i] < largest] or [i for i in range(1, amount) if holding[i] < limit]
        pool, remaining = sum([weights[i] for i in candidates]), surplus
        for i in candidates:
            addition = min(limit - holding[i], max(1, remaining * weights[i] // pool), surplus)
            holding[i] = holding[i] + addition
            surplus = surplus - addition
    return np.array(holding)


def centred(stream_key, extent, width, bound, cuts=(), kind=jnp.bfloat16):
    entries = jax.random.normal(stream_key, extent, jnp.float32) * width
    if len(cuts) > 0:
        entries = levels(stream_key, extent, cuts, -0.22, 0.18) * entries
    return jnp.clip(entries, min=-bound, max=bound).astype(kind)


def setup_inputs(seed: int = 0, part: int = 0) -> dict:
    arg_keys = jax.random.split(jax.random.key(seed), 13)
    part_splits = jax.random.split(jax.random.fold_in(arg_keys[12], part), 13)
    query_rows = draw_query_rows(jax.random.fold_in(jax.random.fold_in(arg_keys[12], part), 71), part)
    key_rows = draw_key_rows(jax.random.fold_in(jax.random.fold_in(arg_keys[12], part), 71), part)
    value_rows = centred(part_splits[2], (PATCHES, VDIM), 1.0, 6.0, ((0, 8), (1, 2)))
    merger_weight = centred(arg_keys[3], (MERGE, VDIM, D), (MERGE * VDIM) ** -0.5, 0.09375, ((1, 2), (2, 8)))
    visual_counts = ragged_sizes(part_splits[4], N_EP, VIS, VCAP, 2).astype(jnp.int32)
    text_rows = centred(part_splits[5], (TEXT, D), 1.0, 6.0, ((0, 8),))
    norm_gain = jnp.clip(1.0 + 0.18 * jax.random.normal(arg_keys[6], (D,), jnp.float32), 0.1, 1.9)
    route_ids_keys = jax.random.split(jax.random.fold_in(part_splits[7], 1), ROWS // SHARE)
    route_ids_turns = jax.random.permutation(jax.random.fold_in(part_splits[7], 3), ROWS // SHARE)
    route_ids = jax.vmap(lambda own, number: shared_out(jax.random.fold_in(part_splits[7], 2), own, number, SHARE, EXPERTS, TOP, CAPACITY, 2))(route_ids_keys, route_ids_turns).reshape((ROWS, TOP))
    route_gates = jnp.clip(jnp.exp(math.log(0.4) - 2.5902672 * jax.random.uniform(part_splits[8], (ROWS, TOP), jnp.float32) ** levels(part_splits[8], (ROWS, TOP), ((0, 8),), -0.2, 0.2)), 0.03, 0.4)
    gate_weight = centred(arg_keys[9], (EXPERTS, D, FF), D ** -0.5, 0.09375, ((0, 8), (2, 2)))
    up_weight = centred(arg_keys[10], (EXPERTS, D, FF), D ** -0.5, 0.09375, ((0, 8), (2, 2)))
    down_weight = centred(arg_keys[11], (EXPERTS, FF, D), FF ** -0.5, 0.21875, ((0, 8), (1, 2)))
    return {"query_rows": query_rows, "key_rows": key_rows, "value_rows": value_rows, "merger_weight": merger_weight, "visual_counts": visual_counts, "text_rows": text_rows, "norm_gain": norm_gain, "route_ids": route_ids, "route_gates": route_gates, "gate_weight": gate_weight, "up_weight": up_weight, "down_weight": down_weight}


def attend_head(triple):
    query_head, key_head, value_head = triple
    scores = jnp.dot(query_head, key_head.T, preferred_element_type=jnp.float32) * HEAD_DIM ** (-0.5)
    weights = jnp.exp(scores - lax.optimization_barrier(jnp.max(scores, axis=1, keepdims=True)))
    mixed = jnp.dot(weights.astype(jnp.bfloat16), value_head, preferred_element_type=jnp.float32)
    return (mixed / lax.optimization_barrier(jnp.sum(weights, axis=1, keepdims=True))).astype(jnp.bfloat16)

def split_heads(matrix):
    return matrix.reshape(PATCHES, HEADS, HEAD_DIM).transpose(1, 0, 2)

def reference(query_rows, key_rows, value_rows, merger_weight, visual_counts, text_rows, norm_gain, route_ids, route_gates, gate_weight, up_weight, down_weight):
    per_head = lax.map(attend_head, (split_heads(query_rows), split_heads(key_rows), split_heads(value_rows)))
    attended = per_head.transpose(1, 0, 2).reshape(PATCHES, VDIM)
    merged = attended.reshape(VIS, MERGE * VDIM)
    visual = jnp.dot(merged, merger_weight.reshape(MERGE * VDIM, D), preferred_element_type=jnp.float32).astype(jnp.bfloat16)
    offsets = jnp.cumsum(visual_counts).astype(jnp.int32) - visual_counts.astype(jnp.int32)
    positions = jnp.arange(VCAP, dtype=jnp.int32)
    filled = positions[None, :] < visual_counts[:, None]
    sources = jnp.clip(offsets[:, None] + positions[None, :], 0, VIS - 1).astype(jnp.int32)
    slot_rows = jnp.where(filled[:, :, None], visual[sources], jnp.zeros((), jnp.bfloat16))
    all_rows = jnp.concatenate([text_rows.reshape(N_EP, LANG_DEV, D), slot_rows], axis=1).reshape(ROWS, D)
    live_rows = jnp.concatenate([jnp.ones((N_EP, LANG_DEV), jnp.bool_), filled], axis=1).reshape(ROWS)
    values = all_rows.astype(jnp.float32)
    normed = (values * lax.rsqrt(lax.optimization_barrier(jnp.mean(values * values, axis=1, keepdims=True)) + 1e-06) * norm_gain).astype(jnp.bfloat16)
    pair_expert = route_ids.reshape(-1)
    pair_live = jnp.repeat(live_rows, TOP)
    pair_gate = route_gates.reshape(-1)
    pair_limit = N_EP * N_TP * CAPACITY

    def one_expert(moe_sum, expert_index):
        chosen = (pair_expert == expert_index) & pair_live
        picked = jnp.nonzero(chosen, size=pair_limit, fill_value=-1)[0].astype(jnp.int32)
        valid = picked >= 0
        safe_pick = jnp.maximum(picked, 0).astype(jnp.int32)
        weight_col = jnp.where(valid, pair_gate[safe_pick], jnp.zeros((), pair_gate.dtype))
        row_index = (safe_pick // TOP).astype(jnp.int32)
        inputs = normed[row_index]
        gate_value = jnp.dot(inputs, gate_weight[expert_index], preferred_element_type=jnp.float32)
        up_value = jnp.dot(inputs, up_weight[expert_index], preferred_element_type=jnp.float32)
        hidden = (jax.nn.silu(gate_value) * up_value).astype(jnp.bfloat16)
        output = jnp.dot(hidden, down_weight[expert_index], preferred_element_type=jnp.float32).astype(jnp.bfloat16)
        return (moe_sum.at[row_index].add(weight_col[:, None] * output.astype(jnp.float32)), None)
    moe_sum, ignored = lax.scan(one_expert, jnp.zeros((ROWS, D), jnp.float32), jnp.arange(EXPERTS, dtype=jnp.int32))
    return (values + moe_sum).astype(jnp.bfloat16)
```

```python
import jax
import jax.numpy as jnp
from jax import lax
from jax.sharding import PartitionSpec as P

HEAD_DIM = 72
MERGE = 4


def attend(query_rows, key_rows, value_rows):
    patch_count = query_rows.shape[0]
    local_heads = query_rows.shape[1] // HEAD_DIM
    score_scale = HEAD_DIM ** (-0.5)
    queries = query_rows.reshape(patch_count, local_heads, HEAD_DIM)
    both = lax.all_gather(jnp.stack([key_rows, value_rows]), "ep", axis=1, tiled=True)
    key_heads = both[0].reshape(-1, local_heads, HEAD_DIM)
    value_heads = both[1].reshape(-1, local_heads, HEAD_DIM)
    scores = (
        jnp.einsum("qhd,khd->hqk", queries, key_heads, preferred_element_type=jnp.float32)
        * score_scale
    )
    weights = jnp.exp(scores - jnp.max(scores, axis=2, keepdims=True))
    sums = jnp.sum(weights, axis=2)
    mixed = jnp.einsum(
        "hqk,khd->hqd", weights.astype(jnp.bfloat16), value_heads, preferred_element_type=jnp.float32
    )
    attended = (mixed / sums[:, :, None]).astype(jnp.bfloat16)
    return attended.transpose(1, 0, 2).reshape(patch_count, local_heads * HEAD_DIM)


def rms(values, norm_gain):
    values = values.astype(jnp.float32)
    scale = lax.rsqrt(jnp.mean(values * values, axis=1, keepdims=True) + 1e-06)
    return (values * scale * norm_gain).astype(jnp.bfloat16)


def body(
    query_rows,
    key_rows,
    value_rows,
    merger_weight,
    visual_counts,
    text_rows,
    norm_gain,
    route_ids,
    route_gates,
    gate_weight,
    up_weight,
    down_weight,
):
    owners = lax.axis_size("ep")
    owner = lax.axis_index("ep")
    patch_count = query_rows.shape[0]
    text_count = text_rows.shape[0]
    row_count = route_ids.shape[0]
    slot_count = row_count - text_count
    local_experts = gate_weight.shape[0]
    expert_count = local_experts * owners
    width = text_rows.shape[1]

    offsets = jnp.cumsum(visual_counts) - visual_counts
    positions = jnp.arange(slot_count, dtype=jnp.int32)
    live = jnp.concatenate(
        [jnp.ones((text_count,), jnp.bool_), positions < visual_counts[owner]]
    )
    named = route_ids[:, :, None] == jnp.arange(expert_count, dtype=jnp.int32)
    grid = jnp.sum(jnp.where(named & live[:, None, None], route_gates[:, :, None], 0.0), axis=1)
    grids = lax.all_to_all(
        grid.reshape(row_count, owners, local_experts).transpose(1, 0, 2),
        "ep", split_axis=0, concat_axis=0, tiled=True,
    )
    sources = offsets[:, None] + positions[None, :]
    filled = positions[None, :] < visual_counts[:, None]
    visual_total = owners * patch_count // MERGE
    pick = (
        filled[:, :, None]
        & (sources[:, :, None] == jnp.arange(visual_total, dtype=jnp.int32))
    )
    text_grid = grids[:, :text_count].reshape(-1, local_experts)
    visual_grid = jnp.einsum(
        "ojv,oje->ve", pick.astype(jnp.float32), grids[:, text_count:],
        precision=lax.Precision.HIGHEST,
    )
    all_grid = jnp.concatenate([text_grid, visual_grid], axis=0)

    text_normed = lax.all_gather(rms(text_rows, norm_gain), "ep", axis=0, tiled=True)

    attended = attend(query_rows, key_rows, value_rows)
    merged = attended.reshape(patch_count // MERGE, -1)
    merged_all = lax.all_gather(merged, "ep", axis=0, tiled=True)
    partial = jnp.dot(
        merged_all, merger_weight.reshape(-1, merger_weight.shape[2]),
        preferred_element_type=jnp.float32,
    )
    half = lax.psum_scatter(partial, "tp", scatter_dimension=0, tiled=True).astype(jnp.bfloat16)
    visual = lax.all_gather(
        lax.all_gather(half, "ep", axis=1, tiled=True), "tp", axis=0, tiled=True
    )
    normed = jnp.concatenate([text_normed, rms(visual, norm_gain)], axis=0)

    total = None
    for e in range(local_experts):
        gate_value = jnp.dot(normed, gate_weight[e], preferred_element_type=jnp.float32)
        up_value = jnp.dot(normed, up_weight[e], preferred_element_type=jnp.float32)
        hidden = jax.nn.silu(gate_value) * up_value * all_grid[:, e : e + 1]
        term = jnp.dot(
            hidden.astype(jnp.bfloat16), down_weight[e], preferred_element_type=jnp.float32
        )
        total = term if total is None else total + term
    total = total.astype(jnp.bfloat16)
    slot_sum = jnp.einsum(
        "ojv,vd->ojd", pick.astype(jnp.bfloat16), total[owners * text_count :],
        preferred_element_type=jnp.float32,
    ).astype(jnp.bfloat16)
    owned = jnp.concatenate(
        [total[: owners * text_count].reshape(owners, text_count, width), slot_sum], axis=1
    ).reshape(-1, width)
    combined = lax.psum_scatter(owned, ("ep", "tp"), scatter_dimension=0, tiled=True)
    my_visual = jnp.dot(
        pick[owner].astype(jnp.bfloat16), visual, preferred_element_type=jnp.float32
    ).astype(jnp.bfloat16)
    rows = jnp.concatenate([text_rows, my_visual], axis=0)
    share = row_count // lax.axis_size("tp")
    residual = lax.dynamic_slice_in_dim(rows, lax.axis_index("tp") * share, share, 0)
    out = (residual.astype(jnp.float32) + combined.astype(jnp.float32)).astype(jnp.bfloat16)
    return lax.all_gather(out, "tp", axis=0, tiled=True)


def solution(mesh):
    return jax.shard_map(
        body,
        mesh=mesh,
        in_specs=(
            P(("grp", "ep"), "tp"),
            P(("grp", "ep"), "tp"),
            P(("grp", "ep"), "tp"),
            P(None, "tp", "ep"),
            P("grp"),
            P(("grp", "ep"), None),
            P(),
            P(("grp", "ep"), None),
            P(("grp", "ep"), None),
            P("ep", None, "tp"),
            P("ep", None, "tp"),
            P("ep", "tp", None),
        ),
        out_specs=P(("grp", "ep"), None),
        check_vma=False,
    )
```

```python
import functools

import jax
import jax.numpy as jnp
from jax import lax
from jax.experimental import pallas as pl
from jax.experimental.pallas import tpu as pltpu
from jax.sharding import PartitionSpec as P

HEAD_DIM = 72
MERGE = 4
MESH = pl.DeviceIdType.MESH
MIB = 1 << 20


class TreeGather:
    def __init__(self, block, count, send_sem, recv_sem):
        self.block, self.send_sem, self.recv_sem = block, send_sem, recv_sem
        me = lax.axis_index("ep")
        self.a, self.b, self.line = me // 2, me % 2, count // 2

    def copy(self, half, a, b, way):
        target = (
            (self.a + 1) * 2 + self.b,
            (self.a - 1) * 2 + self.b,
            self.a * 2 + 1 - self.b,
        )[way]
        target = jnp.clip(target, 0, 2 * self.line - 1)
        slot = a * 2 + b
        return pltpu.make_async_remote_copy(
            src_ref=self.block(half, slot),
            dst_ref=self.block(half, slot),
            send_sem=self.send_sem.at[half, slot, way],
            recv_sem=self.recv_sem.at[half, slot],
            device_id={"ep": target},
            device_id_type=MESH,
        )

    def recv(self, half, a, b):
        self.copy(half, a, b, 2).wait_recv()

    def right(self, half, a, b, act):
        @pl.when(self.a < self.line - 1)
        def _():
            act(self.copy(half, a, b, 0))

    def left(self, half, a, b, act):
        @pl.when(self.a > 0)
        def _():
            act(self.copy(half, a, b, 1))

    def start(self, act=lambda c: c.start()):
        act(self.copy(0, self.a, self.b, 2))
        act(self.copy(1, self.a, self.b, 2))
        for half in range(2):
            self.right(half, self.a, self.b, act)
            self.left(half, self.a, self.b, act)

    def cross(self):
        self.recv(1, self.a, 1 - self.b)
        for go in (self.right, self.left):
            go(1, self.a, 1 - self.b, lambda c: c.start())

    def step(self, d, act=lambda c: c.start(), receive=True):
        for half, column in ((0, self.b), (1, self.b), (1, 1 - self.b)):

            @pl.when(self.a >= d)
            def _():
                if receive:
                    self.recv(half, self.a - d, column)
                self.right(half, self.a - d, column, act)
                if half == 0:
                    act(self.copy(half, self.a - d, column, 2))

            @pl.when(self.a + d < self.line)
            def _():
                if receive:
                    self.recv(half, self.a + d, column)
                self.left(half, self.a + d, column, act)
                if half == 0:
                    act(self.copy(half, self.a + d, column, 2))

    def finish(self):
        for other in range(self.line):
            self.recv(0, other, 1 - self.b)
        wait = lambda c: c.wait_send()
        self.start(wait)
        for go in (self.right, self.left):
            go(1, self.a, 1 - self.b, wait)
        for d in range(1, self.line):
            self.step(d, wait, False)


def greet(count):
    barrier = pltpu.get_barrier_semaphore()
    me, core = lax.axis_index("ep"), lax.axis_index("tp")
    line = count // 2
    a, b = me // 2, me % 2

    def say(ids):
        pl.semaphore_signal(barrier, inc=1, device_id=ids, device_id_type=MESH)

    say({"tp": 1 - core})
    say({"ep": a * 2 + 1 - b})

    @pl.when(a < line - 1)
    def _():
        say({"ep": jnp.minimum(a + 1, line - 1) * 2 + b})

    @pl.when(a > 0)
    def _():
        say({"ep": jnp.maximum(a - 1, 0) * 2 + b})

    edges = jnp.where(a < line - 1, 1, 0) + jnp.where(a > 0, 1, 0)
    pl.semaphore_wait(barrier, 2 + edges)


def to_partner(src, dst, send_sem, recv_sem):
    return pltpu.make_async_remote_copy(
        src_ref=src,
        dst_ref=dst,
        send_sem=send_sem,
        recv_sem=recv_sem,
        device_id={"tp": 1 - lax.axis_index("tp")},
        device_id_type=MESH,
    )


def rms(values, norm_gain):
    values = values.astype(jnp.float32)
    scale = lax.rsqrt(jnp.mean(values * values, axis=1, keepdims=True) + 1e-06)
    return (values * scale * norm_gain).astype(jnp.bfloat16)


def front_kernel(
    count,
    query, key, value, weight, text_ref, gain, grid_ref,
    normed_out, visual_out, grid_out,
    kv, text, att, vis, grid, part, part_in,
    kv_send, kv_recv, text_send, text_recv, att_send, att_recv, vis_send, vis_recv,
    grid_send, grid_recv, pair_send, pair_recv,
):
    me, core = lax.axis_index("ep"), lax.axis_index("tp")
    line = count // 2
    kv_gather = TreeGather(lambda h, s: kv.at[h, s], count, kv_send, kv_recv)
    text_gather = TreeGather(lambda h, s: text.at[core, h, s], count, text_send, text_recv)
    att_gather = TreeGather(lambda h, s: att.at[h, s], count, att_send, att_recv)
    vis_gather = TreeGather(lambda h, s: vis.at[core, h, s], count, vis_send, vis_recv)
    grid_gather = TreeGather(lambda h, s: grid.at[h, s], count, grid_send, grid_recv)

    kv[0, me] = key[...]
    kv[1, me] = value[...]
    greet(count)
    kv_gather.start()
    width = text_ref.shape[1]
    mine = text_ref.shape[0] // 2
    own = rms(text_ref[pl.ds(pl.multiple_of(core * mine, mine), mine), :], gain[...])
    text[core, 0, me] = own[:, : width // 2]
    text[core, 1, me] = own[:, width // 2 :]
    grid[0, me] = grid_ref[0]
    grid[1, me] = grid_ref[1]
    kv_gather.cross()
    for d in range(1, line):
        kv_gather.step(d)
        if d == 1:
            grid_gather.start()
            text_gather.start()
    kv_gather.finish()
    grid_gather.cross()
    text_gather.cross()
    text_gather.step(1)
    grid_gather.step(1)

    patches, features = query.shape
    keys = kv[0].reshape(count * patches, features)
    values = kv[1].reshape(count * patches, features)
    parts = []
    for head in range(features // HEAD_DIM):
        lanes = slice(head * HEAD_DIM, (head + 1) * HEAD_DIM)
        scores = lax.dot_general(
            query[:, lanes], keys[:, lanes], (((1,), (1,)), ((), ())),
            preferred_element_type=jnp.float32,
        ) * (HEAD_DIM ** (-0.5))
        weights = jnp.exp(scores - jnp.max(scores, axis=1, keepdims=True))
        sums = jnp.sum(weights, axis=1, keepdims=True)
        mixed = jnp.dot(
            weights.astype(jnp.bfloat16), values[:, lanes], preferred_element_type=jnp.float32
        )
        parts.append((mixed / sums).astype(jnp.bfloat16))
    attended = jnp.concatenate(parts, axis=1)
    rows = patches // MERGE
    for p in range(MERGE):
        att[p // 2, me, p % 2] = attended[p * rows : (p + 1) * rows]
    att_gather.start()
    late = [d for d in range(2, line)]
    for d in late[: len(late) // 2]:
        text_gather.step(d)
    att_gather.cross()
    for d in range(1, line):
        att_gather.step(d)
    for d in late[len(late) // 2 :]:
        text_gather.step(d)
    for d in late:
        grid_gather.step(d)
    att_gather.finish()

    total = None
    for p in range(MERGE):
        left = att[p // 2, :, p % 2].reshape(count * rows, features)
        term = jnp.dot(left, weight[p], preferred_element_type=jnp.float32)
        total = term if total is None else total + term
    half_rows = count * rows // 2
    part[0] = total[:half_rows]
    part[1] = total[half_rows:]
    swap = to_partner(part.at[1 - core], part_in, pair_send.at[0], pair_recv.at[0])
    swap.start()
    swap.wait()
    summed = (part[core] + part_in[...]).astype(jnp.bfloat16)
    quarter = half_rows // 2
    vis[core, 0, me] = summed[:quarter]
    vis[core, 1, me] = summed[quarter:]
    vis_gather.start()
    text_gather.finish()
    swap_text = to_partner(text.at[core], text.at[core], pair_send.at[1], pair_recv.at[1])
    swap_text.start()
    vis_gather.cross()
    for d in range(1, line):
        vis_gather.step(d)
    grid_gather.finish()
    for s in range(count):
        for h in range(2):
            grid_out[s, h] = grid[h, s]
    vis_gather.finish()
    swap_vis = to_partner(vis.at[core], vis.at[core], pair_send.at[2], pair_recv.at[2])
    swap_vis.start()
    swap_text.wait_send()
    to_partner(text.at[1 - core], text.at[1 - core], pair_send.at[1], pair_recv.at[1]).wait_recv()
    for s in range(count):
        for c in range(2):
            for h in range(2):
                normed_out[
                    s * 2 * mine + c * mine : s * 2 * mine + (c + 1) * mine,
                    h * width // 2 : (h + 1) * width // 2,
                ] = text[c, h, s]
    swap_vis.wait_send()
    to_partner(vis.at[1 - core], vis.at[1 - core], pair_send.at[2], pair_recv.at[2]).wait_recv()
    columns = weight.shape[2]
    base = count * 2 * mine
    for c in range(2):
        for h in range(2):
            first = (c * 2 + h) * quarter
            for s in range(count):
                visual_out[first : first + quarter, s * columns : (s + 1) * columns] = vis[c, h, s]
            normed_out[base + first : base + first + quarter, :] = rms(
                visual_out[first : first + quarter, :], gain[...]
            )


def front(query_rows, key_rows, value_rows, merger_weight, text_rows, norm_gain, grid):
    count = lax.axis_size("ep")
    patches, features = query_rows.shape
    rows = patches // MERGE
    text_count, width = text_rows.shape
    columns = merger_weight.shape[2]
    quarter = count * rows // 4
    queries = query_rows.reshape(rows, MERGE, features).transpose(1, 0, 2).reshape(patches, features)
    bf16, f32 = jnp.bfloat16, jnp.float32
    sems = []
    for _ in range(5):
        sems += [pltpu.SemaphoreType.DMA((2, count, 3)), pltpu.SemaphoreType.DMA((2, count))]
    vmem = pl.BlockSpec(memory_space=pltpu.VMEM)
    return pl.pallas_call(
        functools.partial(front_kernel, count),
        name="front",
        out_shape=(
            jax.ShapeDtypeStruct((count * (text_count + rows), width), bf16),
            jax.ShapeDtypeStruct((count * rows, width), bf16),
            jax.ShapeDtypeStruct((count,) + grid.shape, f32),
        ),
        in_specs=[vmem] * 7,
        out_specs=(vmem,) * 3,
        scratch_shapes=[
            pltpu.VMEM((2, count, patches, features), bf16),
            pltpu.VMEM((2, 2, count, text_count // 2, width // 2), bf16),
            pltpu.VMEM((2, count, 2, rows, features), bf16),
            pltpu.VMEM((2, 2, count, quarter, columns), bf16),
            pltpu.VMEM((2, count) + grid.shape[1:], f32),
            pltpu.VMEM((2, 2 * quarter, columns), f32),
            pltpu.VMEM((2 * quarter, columns), f32),
        ]
        + sems
        + [pltpu.SemaphoreType.DMA((3,)), pltpu.SemaphoreType.DMA((3,))],
        compiler_params=pltpu.CompilerParams(
            collective_id=0, has_side_effects=True, vmem_limit_bytes=56 * MIB
        ),
    )(queries, key_rows, value_rows, merger_weight, text_rows, norm_gain.reshape(1, -1), grid)


def body(
    query_rows,
    key_rows,
    value_rows,
    merger_weight,
    visual_counts,
    text_rows,
    norm_gain,
    route_ids,
    route_gates,
    gate_weight,
    up_weight,
    down_weight,
):
    owners = lax.axis_size("ep")
    owner = lax.axis_index("ep")
    patch_count = query_rows.shape[0]
    text_count = text_rows.shape[0]
    row_count = route_ids.shape[0]
    slot_count = row_count - text_count
    local_experts = gate_weight.shape[0]
    expert_count = local_experts * owners
    width = text_rows.shape[1]

    offsets = jnp.cumsum(visual_counts) - visual_counts
    positions = jnp.arange(slot_count, dtype=jnp.int32)
    live = jnp.concatenate(
        [jnp.ones((text_count,), jnp.bool_), positions < visual_counts[owner]]
    )
    named = route_ids[:, :, None] == jnp.arange(expert_count, dtype=jnp.int32)
    grid = jnp.sum(jnp.where(named & live[:, None, None], route_gates[:, :, None], 0.0), axis=1)
    flat = jnp.pad(grid.T, ((0, 0), (0, -row_count % 128)))
    flat = flat.reshape(2, expert_count // 2, -1)
    normed, visual, grids = front(
        query_rows, key_rows, value_rows, merger_weight, text_rows, norm_gain, flat
    )
    grids = grids.reshape(owners, owners, local_experts, -1)
    grids = lax.dynamic_index_in_dim(grids, owner, 1, False)[:, :, :row_count]
    grids = grids.transpose(0, 2, 1)
    sources = offsets[:, None] + positions[None, :]
    filled = positions[None, :] < visual_counts[:, None]
    visual_total = owners * patch_count // MERGE
    pick = (
        filled[:, :, None]
        & (sources[:, :, None] == jnp.arange(visual_total, dtype=jnp.int32))
    )
    text_grid = grids[:, :text_count].reshape(-1, local_experts)
    visual_grid = jnp.einsum(
        "ojv,oje->ve", pick.astype(jnp.float32), grids[:, text_count:],
        precision=lax.Precision.HIGHEST,
    )
    all_grid = jnp.concatenate([text_grid, visual_grid], axis=0)

    total = None
    for e in range(local_experts):
        gate_value = jnp.dot(normed, gate_weight[e], preferred_element_type=jnp.float32)
        up_value = jnp.dot(normed, up_weight[e], preferred_element_type=jnp.float32)
        hidden = jax.nn.silu(gate_value) * up_value * all_grid[:, e : e + 1]
        term = jnp.dot(
            hidden.astype(jnp.bfloat16), down_weight[e], preferred_element_type=jnp.float32
        )
        total = term if total is None else total + term
    total = total.astype(jnp.bfloat16)
    slot_sum = jnp.einsum(
        "ojv,vd->ojd", pick.astype(jnp.bfloat16), total[owners * text_count :],
        preferred_element_type=jnp.float32,
    ).astype(jnp.bfloat16)
    owned = jnp.concatenate(
        [total[: owners * text_count].reshape(owners, text_count, width), slot_sum], axis=1
    ).reshape(-1, width)
    combined = lax.psum_scatter(owned, ("ep", "tp"), scatter_dimension=0, tiled=True)
    my_visual = jnp.dot(
        pick[owner].astype(jnp.bfloat16), visual, preferred_element_type=jnp.float32
    ).astype(jnp.bfloat16)
    rows = jnp.concatenate([text_rows, my_visual], axis=0)
    share = row_count // lax.axis_size("tp")
    residual = lax.dynamic_slice_in_dim(rows, lax.axis_index("tp") * share, share, 0)
    out = (residual.astype(jnp.float32) + combined.astype(jnp.float32)).astype(jnp.bfloat16)
    return lax.all_gather(out, "tp", axis=0, tiled=True)


def solution(mesh):
    return jax.shard_map(
        body,
        mesh=mesh,
        in_specs=(
            P(("grp", "ep"), "tp"),
            P(("grp", "ep"), "tp"),
            P(("grp", "ep"), "tp"),
            P(None, "tp", "ep"),
            P("grp"),
            P(("grp", "ep"), None),
            P(),
            P(("grp", "ep"), None),
            P(("grp", "ep"), None),
            P("ep", None, "tp"),
            P("ep", None, "tp"),
            P("ep", "tp", None),
        ),
        out_specs=P(("grp", "ep"), None),
        check_vma=False,
    )
```

```python
import functools

import jax
import jax.numpy as jnp
from jax import lax
from jax.experimental import pallas as pl
from jax.experimental.pallas import tpu as pltpu
from jax.sharding import PartitionSpec as P

HEAD_DIM = 72
MERGE = 4
MESH = pl.DeviceIdType.MESH
MIB = 1 << 20


class TreeGather:
    def __init__(self, block, count, send_sem, recv_sem):
        self.block, self.send_sem, self.recv_sem = block, send_sem, recv_sem
        me = lax.axis_index("ep")
        self.a, self.b, self.line = me // 2, me % 2, count // 2

    def copy(self, half, a, b, way):
        target = (
            (self.a + 1) * 2 + self.b,
            (self.a - 1) * 2 + self.b,
            self.a * 2 + 1 - self.b,
        )[way]
        target = jnp.clip(target, 0, 2 * self.line - 1)
        slot = a * 2 + b
        return pltpu.make_async_remote_copy(
            src_ref=self.block(half, slot),
            dst_ref=self.block(half, slot),
            send_sem=self.send_sem.at[half, slot, way],
            recv_sem=self.recv_sem.at[half, slot],
            device_id={"ep": target},
            device_id_type=MESH,
        )

    def recv(self, half, a, b):
        self.copy(half, a, b, 2).wait_recv()

    def right(self, half, a, b, act):
        @pl.when(self.a < self.line - 1)
        def _():
            act(self.copy(half, a, b, 0))

    def left(self, half, a, b, act):
        @pl.when(self.a > 0)
        def _():
            act(self.copy(half, a, b, 1))

    def start(self, act=lambda c: c.start()):
        act(self.copy(0, self.a, self.b, 2))
        act(self.copy(1, self.a, self.b, 2))
        for half in range(2):
            self.right(half, self.a, self.b, act)
            self.left(half, self.a, self.b, act)

    def cross(self):
        self.recv(1, self.a, 1 - self.b)
        for go in (self.right, self.left):
            go(1, self.a, 1 - self.b, lambda c: c.start())

    def step(self, d, act=lambda c: c.start(), receive=True):
        for half, column in ((0, self.b), (1, self.b), (1, 1 - self.b)):

            @pl.when(self.a >= d)
            def _():
                if receive:
                    self.recv(half, self.a - d, column)
                self.right(half, self.a - d, column, act)
                if half == 0:
                    act(self.copy(half, self.a - d, column, 2))

            @pl.when(self.a + d < self.line)
            def _():
                if receive:
                    self.recv(half, self.a + d, column)
                self.left(half, self.a + d, column, act)
                if half == 0:
                    act(self.copy(half, self.a + d, column, 2))

    def finish(self):
        for other in range(self.line):
            self.recv(0, other, 1 - self.b)
        wait = lambda c: c.wait_send()
        self.start(wait)
        for go in (self.right, self.left):
            go(1, self.a, 1 - self.b, wait)
        for d in range(1, self.line):
            self.step(d, wait, False)


def greet(count):
    barrier = pltpu.get_barrier_semaphore()
    me, core = lax.axis_index("ep"), lax.axis_index("tp")
    line = count // 2
    a, b = me // 2, me % 2

    def say(ids):
        pl.semaphore_signal(barrier, inc=1, device_id=ids, device_id_type=MESH)

    say({"tp": 1 - core})
    say({"ep": a * 2 + 1 - b})

    @pl.when(a < line - 1)
    def _():
        say({"ep": jnp.minimum(a + 1, line - 1) * 2 + b})

    @pl.when(a > 0)
    def _():
        say({"ep": jnp.maximum(a - 1, 0) * 2 + b})

    edges = jnp.where(a < line - 1, 1, 0) + jnp.where(a > 0, 1, 0)
    pl.semaphore_wait(barrier, 2 + edges)


def to_partner(src, dst, send_sem, recv_sem):
    return pltpu.make_async_remote_copy(
        src_ref=src,
        dst_ref=dst,
        send_sem=send_sem,
        recv_sem=recv_sem,
        device_id={"tp": 1 - lax.axis_index("tp")},
        device_id_type=MESH,
    )


def rms(values, norm_gain):
    values = values.astype(jnp.float32)
    scale = lax.rsqrt(jnp.mean(values * values, axis=1, keepdims=True) + 1e-06)
    return (values * scale * norm_gain).astype(jnp.bfloat16)


def front_kernel(
    count,
    query, key, value, weight, text_ref, gain, grid_ref,
    normed_out, visual_out, grid_out,
    kv, text, att, vis, grid, part, part_in,
    kv_send, kv_recv, text_send, text_recv, att_send, att_recv, vis_send, vis_recv,
    grid_send, grid_recv, pair_send, pair_recv,
):
    me, core = lax.axis_index("ep"), lax.axis_index("tp")
    line = count // 2
    kv_gather = TreeGather(lambda h, s: kv.at[h, s], count, kv_send, kv_recv)
    text_gather = TreeGather(lambda h, s: text.at[core, h, s], count, text_send, text_recv)
    att_gather = TreeGather(lambda h, s: att.at[h, s], count, att_send, att_recv)
    vis_gather = TreeGather(lambda h, s: vis.at[core, h, s], count, vis_send, vis_recv)
    grid_gather = TreeGather(lambda h, s: grid.at[h, s], count, grid_send, grid_recv)

    kv[0, me] = key[...]
    kv[1, me] = value[...]
    greet(count)
    kv_gather.start()
    width = text_ref.shape[1]
    mine = text_ref.shape[0] // 2
    own = rms(text_ref[pl.ds(pl.multiple_of(core * mine, mine), mine), :], gain[...])
    text[core, 0, me] = own[:, : width // 2]
    text[core, 1, me] = own[:, width // 2 :]
    grid[0, me] = grid_ref[0]
    grid[1, me] = grid_ref[1]
    kv_gather.cross()
    for d in range(1, line):
        kv_gather.step(d)
        if d == 1:
            grid_gather.start()
            text_gather.start()
    kv_gather.finish()
    grid_gather.cross()
    text_gather.cross()
    text_gather.step(1)
    grid_gather.step(1)

    patches, features = query.shape
    keys = kv[0].reshape(count * patches, features)
    values = kv[1].reshape(count * patches, features)
    parts = []
    for head in range(features // HEAD_DIM):
        lanes = slice(head * HEAD_DIM, (head + 1) * HEAD_DIM)
        scores = lax.dot_general(
            query[:, lanes], keys[:, lanes], (((1,), (1,)), ((), ())),
            preferred_element_type=jnp.float32,
        ) * (HEAD_DIM ** (-0.5))
        weights = jnp.exp(scores - jnp.max(scores, axis=1, keepdims=True))
        sums = jnp.sum(weights, axis=1, keepdims=True)
        mixed = jnp.dot(
            weights.astype(jnp.bfloat16), values[:, lanes], preferred_element_type=jnp.float32
        )
        parts.append((mixed / sums).astype(jnp.bfloat16))
    attended = jnp.concatenate(parts, axis=1)
    rows = patches // MERGE
    for p in range(MERGE):
        att[p // 2, me, p % 2] = attended[p * rows : (p + 1) * rows]
    att_gather.start()
    late = [d for d in range(2, line)]
    for d in late[: len(late) // 2]:
        text_gather.step(d)
    att_gather.cross()
    for d in range(1, line):
        att_gather.step(d)
    for d in late[len(late) // 2 :]:
        text_gather.step(d)
    for d in late:
        grid_gather.step(d)
    att_gather.finish()

    total = None
    for p in range(MERGE):
        left = att[p // 2, :, p % 2].reshape(count * rows, features)
        term = jnp.dot(left, weight[p], preferred_element_type=jnp.float32)
        total = term if total is None else total + term
    half_rows = count * rows // 2
    part[0] = total[:half_rows]
    part[1] = total[half_rows:]
    swap = to_partner(part.at[1 - core], part_in, pair_send.at[0], pair_recv.at[0])
    swap.start()
    swap.wait()
    summed = (part[core] + part_in[...]).astype(jnp.bfloat16)
    quarter = half_rows // 2
    vis[core, 0, me] = summed[:quarter]
    vis[core, 1, me] = summed[quarter:]
    vis_gather.start()
    text_gather.finish()
    swap_text = to_partner(text.at[core], text.at[core], pair_send.at[1], pair_recv.at[1])
    swap_text.start()
    vis_gather.cross()
    for d in range(1, line):
        vis_gather.step(d)
    grid_gather.finish()
    for s in range(count):
        for h in range(2):
            grid_out[s, h] = grid[h, s]
    vis_gather.finish()
    swap_vis = to_partner(vis.at[core], vis.at[core], pair_send.at[2], pair_recv.at[2])
    swap_vis.start()
    swap_text.wait_send()
    to_partner(text.at[1 - core], text.at[1 - core], pair_send.at[1], pair_recv.at[1]).wait_recv()
    for s in range(count):
        for c in range(2):
            for h in range(2):
                normed_out[
                    s * 2 * mine + c * mine : s * 2 * mine + (c + 1) * mine,
                    h * width // 2 : (h + 1) * width // 2,
                ] = text[c, h, s]
    swap_vis.wait_send()
    to_partner(vis.at[1 - core], vis.at[1 - core], pair_send.at[2], pair_recv.at[2]).wait_recv()
    columns = weight.shape[2]
    base = count * 2 * mine
    for c in range(2):
        for h in range(2):
            first = (c * 2 + h) * quarter
            for s in range(count):
                visual_out[first : first + quarter, s * columns : (s + 1) * columns] = vis[c, h, s]
            normed_out[base + first : base + first + quarter, :] = rms(
                visual_out[first : first + quarter, :], gain[...]
            )


def front(query_rows, key_rows, value_rows, merger_weight, text_rows, norm_gain, grid):
    count = lax.axis_size("ep")
    patches, features = query_rows.shape
    rows = patches // MERGE
    text_count, width = text_rows.shape
    columns = merger_weight.shape[2]
    quarter = count * rows // 4
    queries = query_rows.reshape(rows, MERGE, features).transpose(1, 0, 2).reshape(patches, features)
    bf16, f32 = jnp.bfloat16, jnp.float32
    sems = []
    for _ in range(5):
        sems += [pltpu.SemaphoreType.DMA((2, count, 3)), pltpu.SemaphoreType.DMA((2, count))]
    vmem = pl.BlockSpec(memory_space=pltpu.VMEM)
    return pl.pallas_call(
        functools.partial(front_kernel, count),
        name="front",
        out_shape=(
            jax.ShapeDtypeStruct((count * (text_count + rows), width), bf16),
            jax.ShapeDtypeStruct((count * rows, width), bf16),
            jax.ShapeDtypeStruct((count,) + grid.shape, f32),
        ),
        in_specs=[vmem] * 7,
        out_specs=(vmem,) * 3,
        scratch_shapes=[
            pltpu.VMEM((2, count, patches, features), bf16),
            pltpu.VMEM((2, 2, count, text_count // 2, width // 2), bf16),
            pltpu.VMEM((2, count, 2, rows, features), bf16),
            pltpu.VMEM((2, 2, count, quarter, columns), bf16),
            pltpu.VMEM((2, count) + grid.shape[1:], f32),
            pltpu.VMEM((2, 2 * quarter, columns), f32),
            pltpu.VMEM((2 * quarter, columns), f32),
        ]
        + sems
        + [pltpu.SemaphoreType.DMA((3,)), pltpu.SemaphoreType.DMA((3,))],
        compiler_params=pltpu.CompilerParams(
            collective_id=0, has_side_effects=True, vmem_limit_bytes=56 * MIB
        ),
    )(queries, key_rows, value_rows, merger_weight, text_rows, norm_gain.reshape(1, -1), grid)


def back_kernel(
    count,
    normed, gates, pick, gate_hbm, up_hbm, down_hbm,
    out_ref,
    pair_w, down, hidden, acc, pin, cross0, cross1, zin, fin,
    load_sem, down_sem, pair_send, pair_recv, y_send, y_recv, z_send, z_recv,
):
    core, me = lax.axis_index("tp"), lax.axis_index("ep")
    line = count // 2
    a, b = me // 2, me % 2
    experts, width, units = gate_hbm.shape
    total_rows = normed.shape[0]
    visual = pick.shape[1]
    texts = (total_rows - visual) // count
    slots = pick.shape[0] // count
    span = acc.shape[4]
    slot_total = pair_w.shape[0]
    step_rows = 384 if total_rows % 384 == 0 else total_rows

    def load(e, which):
        slot = e % slot_total
        source = (gate_hbm, up_hbm)[which]
        return pltpu.make_async_copy(
            source.at[e], pair_w.at[slot, :, pl.ds(which * units, units)], load_sem.at[slot, which]
        )

    def load_down(e):
        return pltpu.make_async_copy(
            down_hbm.at[e], down.at[pl.ds(e * units, units), :], down_sem.at[e]
        )

    for e in range(slot_total):
        load(e, 0).start()
        load(e, 1).start()
    for e in range(experts):
        load_down(e).start()
    greet(count)

    @pl.loop(0, experts)
    def _(e):
        load(e, 0).wait()
        load(e, 1).wait()
        for first in range(0, total_rows, step_rows):
            rows = slice(first, first + step_rows)
            both = jnp.dot(
                normed[rows, :], pair_w[e % slot_total], preferred_element_type=jnp.float32
            )
            value = both[:, :units]
            gated = value / (1.0 + jnp.exp(-value)) * both[:, units:] * gates[e, rows, :]
            hidden[rows, pl.ds(pl.multiple_of(e * units, 128), units)] = gated.astype(jnp.bfloat16)

        @pl.when(e + slot_total < experts)
        def _():
            load(e + slot_total, 0).start()
            load(e + slot_total, 1).start()

    for e in range(experts):
        load_down(e).wait()
    chunk = 512
    base = total_rows - visual

    def half_sums(side, half, add):
        for offset in range(0, span, chunk):
            start = pl.multiple_of(side * 2 * span + half * span + offset, chunk)
            weight = down[:, pl.ds(start, chunk)]
            lanes = slice(offset, offset + chunk)
            text = jnp.dot(hidden[:base, :], weight, preferred_element_type=jnp.float32)
            seen = jnp.dot(hidden[base:, :], weight, preferred_element_type=jnp.float32)
            placed = jnp.dot(
                pick[...], seen.astype(jnp.bfloat16), preferred_element_type=jnp.float32
            )
            for s in range(count):
                sums = jnp.concatenate(
                    [text[s * texts : (s + 1) * texts], placed[s * slots : (s + 1) * slots]]
                )
                if add:
                    sums = sums + pin[half, s % 2, s // 2, :, lanes].astype(jnp.float32)
                acc[half, s % 2, s // 2, :, lanes] = sums.astype(jnp.bfloat16)

    swaps = [
        to_partner(acc.at[h], pin.at[h], pair_send.at[h], pair_recv.at[h]) for h in range(2)
    ]
    for h in range(2):
        half_sums(1 - core, h, False)
        swaps[h].start()

    def remote(src, dst, send_sem, recv_sem, target):
        return pltpu.make_async_remote_copy(
            src_ref=src, dst_ref=dst, send_sem=send_sem, recv_sem=recv_sem,
            device_id={"ep": target}, device_id_type=MESH,
        )

    other = a * 2 + 1 - b
    swaps[0].wait()
    half_sums(core, 0, True)
    first_cross = remote(acc.at[0, 1 - b], cross0, y_send.at[0], y_recv.at[0], other)
    first_cross.start()
    swaps[1].wait()
    half_sums(core, 1, True)

    places = ((0, b), (1, b), (1, 1 - b))

    def hop(q, target, way):
        half, column = places[q]
        towards = jnp.clip(a + (1, -1)[way], 0, line - 1) * 2 + b
        return remote(
            acc.at[half, column, target], zin.at[q, target + 1 - way],
            z_send.at[q, target, way], z_recv.at[q, target, way], towards,
        )

    def take(q, target, way):
        half, column = places[q]
        hop(q, target, way).wait_recv()
        acc[half, column, target] = (
            acc[half, column, target].astype(jnp.float32)
            + zin[q, target + 1 - way].astype(jnp.float32)
        ).astype(jnp.bfloat16)

    def flow(q, i):
        right, left = line - 1 - i, i

        @pl.when(right > a)
        def _():
            @pl.when(a > 0)
            def _():
                take(q, right, 0)

            hop(q, right, 0).start()

        @pl.when(left < a)
        def _():
            @pl.when(a < line - 1)
            def _():
                take(q, left, 1)

            hop(q, left, 1).start()

    def land(q):
        @pl.when(a > 0)
        def _():
            take(q, a, 0)

        @pl.when(a < line - 1)
        def _():
            take(q, a, 1)

    flow(2, 0)
    flow(1, 0)
    first_cross.wait()
    for t in range(line):
        acc[0, b, t] = (
            acc[0, b, t].astype(jnp.float32) + cross0[t].astype(jnp.float32)
        ).astype(jnp.bfloat16)
    flow(0, 0)
    for i in range(1, line - 1):
        for q in (2, 1, 0):
            flow(q, i)
    land(2)
    last_cross = remote(acc.at[1, 1 - b, a], cross1, y_send.at[1], y_recv.at[1], other)
    last_cross.start()
    land(1)
    land(0)
    fin[core, 0] = acc[0, b, a]
    last_cross.wait()
    fin[core, 1] = (
        acc[1, b, a].astype(jnp.float32) + cross1[...].astype(jnp.float32)
    ).astype(jnp.bfloat16)
    to_partner(fin.at[core], fin.at[core], pair_send.at[2], pair_recv.at[2]).start()
    for q in range(3):
        for t in range(line):

            @pl.when(t > a)
            def _():
                hop(q, t, 0).wait_send()

            @pl.when(t < a)
            def _():
                hop(q, t, 1).wait_send()

    to_partner(fin.at[core], fin.at[core], pair_send.at[2], pair_recv.at[2]).wait_send()
    to_partner(fin.at[1 - core], fin.at[1 - core], pair_send.at[2], pair_recv.at[2]).wait_recv()
    for c in range(2):
        for h in range(2):
            out_ref[:, (c * 2 + h) * span : (c * 2 + h + 1) * span] = fin[c, h]


def back(normed, gates, pick, gate_weight, up_weight, down_weight):
    count = lax.axis_size("ep")
    line = count // 2
    experts, width, units = gate_weight.shape
    total_rows = normed.shape[0]
    owned = (total_rows - pick.shape[1] + pick.shape[0]) // count
    span = width // 4
    bf16 = jnp.bfloat16
    dma = pltpu.SemaphoreType.DMA
    vmem, hbm = pl.BlockSpec(memory_space=pltpu.VMEM), pl.BlockSpec(memory_space=pl.ANY)
    return pl.pallas_call(
        functools.partial(back_kernel, count),
        name="back",
        out_shape=jax.ShapeDtypeStruct((owned, width), bf16),
        in_specs=[vmem] * 3 + [hbm] * 3,
        out_specs=vmem,
        scratch_shapes=[
            pltpu.VMEM((min(2, experts), width, 2 * units), bf16),
            pltpu.VMEM((experts * units, width), bf16),
            pltpu.VMEM((total_rows, experts * units), bf16),
            pltpu.VMEM((2, 2, line, owned, span), bf16),
            pltpu.VMEM((2, 2, line, owned, span), bf16),
            pltpu.VMEM((line, owned, span), bf16),
            pltpu.VMEM((owned, span), bf16),
            pltpu.VMEM((3, line + 1, owned, span), bf16),
            pltpu.VMEM((2, 2, owned, span), bf16),
            dma((2, 2)), dma((experts,)), dma((3,)), dma((3,)), dma((2,)), dma((2,)),
            dma((3, line, 2)), dma((3, line, 2)),
        ],
        compiler_params=pltpu.CompilerParams(
            collective_id=1, has_side_effects=True, vmem_limit_bytes=62 * MIB
        ),
    )(normed, gates, pick, gate_weight, up_weight, down_weight)


def body(
    query_rows,
    key_rows,
    value_rows,
    merger_weight,
    visual_counts,
    text_rows,
    norm_gain,
    route_ids,
    route_gates,
    gate_weight,
    up_weight,
    down_weight,
):
    owners = lax.axis_size("ep")
    owner = lax.axis_index("ep")
    patch_count = query_rows.shape[0]
    text_count = text_rows.shape[0]
    row_count = route_ids.shape[0]
    slot_count = row_count - text_count
    local_experts = gate_weight.shape[0]
    expert_count = local_experts * owners
    width = text_rows.shape[1]

    offsets = jnp.cumsum(visual_counts) - visual_counts
    positions = jnp.arange(slot_count, dtype=jnp.int32)
    live = jnp.concatenate(
        [jnp.ones((text_count,), jnp.bool_), positions < visual_counts[owner]]
    )
    named = route_ids[:, :, None] == jnp.arange(expert_count, dtype=jnp.int32)
    grid = jnp.sum(jnp.where(named & live[:, None, None], route_gates[:, :, None], 0.0), axis=1)
    flat = jnp.pad(grid.T, ((0, 0), (0, -row_count % 128)))
    flat = flat.reshape(2, expert_count // 2, -1)
    normed, visual, grids = front(
        query_rows, key_rows, value_rows, merger_weight, text_rows, norm_gain, flat
    )
    grids = grids.reshape(owners, owners, local_experts, -1)
    grids = lax.dynamic_index_in_dim(grids, owner, 1, False)[:, :, :row_count]
    grids = grids.transpose(0, 2, 1)
    sources = offsets[:, None] + positions[None, :]
    filled = positions[None, :] < visual_counts[:, None]
    visual_total = owners * patch_count // MERGE
    pick = (
        filled[:, :, None]
        & (sources[:, :, None] == jnp.arange(visual_total, dtype=jnp.int32))
    )
    text_grid = grids[:, :text_count].reshape(-1, local_experts)
    visual_grid = jnp.einsum(
        "ojv,oje->ve", pick.astype(jnp.float32), grids[:, text_count:],
        precision=lax.Precision.HIGHEST,
    )
    all_grid = jnp.concatenate([text_grid, visual_grid], axis=0)

    combined = back(
        normed,
        all_grid.T[:, :, None],
        pick.reshape(owners * slot_count, visual_total).astype(jnp.bfloat16),
        gate_weight,
        up_weight,
        down_weight,
    )
    my_visual = jnp.dot(
        pick[owner].astype(jnp.bfloat16), visual, preferred_element_type=jnp.float32
    ).astype(jnp.bfloat16)
    rows = jnp.concatenate([text_rows, my_visual], axis=0)
    return (rows.astype(jnp.float32) + combined.astype(jnp.float32)).astype(jnp.bfloat16)


def solution(mesh):
    return jax.shard_map(
        body,
        mesh=mesh,
        in_specs=(
            P(("grp", "ep"), "tp"),
            P(("grp", "ep"), "tp"),
            P(("grp", "ep"), "tp"),
            P(None, "tp", "ep"),
            P("grp"),
            P(("grp", "ep"), None),
            P(),
            P(("grp", "ep"), None),
            P(("grp", "ep"), None),
            P("ep", None, "tp"),
            P("ep", None, "tp"),
            P("ep", "tp", None),
        ),
        out_specs=P(("grp", "ep"), None),
        check_vma=False,
    )
```

```python
import functools

import jax
import jax.numpy as jnp
from jax import lax
from jax.experimental import pallas as pl
from jax.experimental.pallas import tpu as pltpu
from jax.sharding import PartitionSpec as P

HEAD_DIM = 72
MERGE = 4
MESH = pl.DeviceIdType.MESH
MIB = 1 << 20


class TreeGather:
    def __init__(self, block, count, send_sem, recv_sem):
        self.block, self.send_sem, self.recv_sem = block, send_sem, recv_sem
        me = lax.axis_index("ep")
        self.a, self.b, self.line = me // 2, me % 2, count // 2

    def copy(self, half, a, b, way):
        target = (
            (self.a + 1) * 2 + self.b,
            (self.a - 1) * 2 + self.b,
            self.a * 2 + 1 - self.b,
        )[way]
        target = jnp.clip(target, 0, 2 * self.line - 1)
        slot = a * 2 + b
        return pltpu.make_async_remote_copy(
            src_ref=self.block(half, slot),
            dst_ref=self.block(half, slot),
            send_sem=self.send_sem.at[half, slot, way],
            recv_sem=self.recv_sem.at[half, slot],
            device_id={"ep": target},
            device_id_type=MESH,
        )

    def recv(self, half, a, b):
        self.copy(half, a, b, 2).wait_recv()

    def right(self, half, a, b, act):
        @pl.when(self.a < self.line - 1)
        def _():
            act(self.copy(half, a, b, 0))

    def left(self, half, a, b, act):
        @pl.when(self.a > 0)
        def _():
            act(self.copy(half, a, b, 1))

    def start(self, act=lambda c: c.start()):
        act(self.copy(0, self.a, self.b, 2))
        act(self.copy(1, self.a, self.b, 2))
        for half in range(2):
            self.right(half, self.a, self.b, act)
            self.left(half, self.a, self.b, act)

    def cross(self):
        self.recv(1, self.a, 1 - self.b)
        for go in (self.right, self.left):
            go(1, self.a, 1 - self.b, lambda c: c.start())

    def step(self, d, act=lambda c: c.start(), receive=True):
        for half, column in ((0, self.b), (1, self.b), (1, 1 - self.b)):

            @pl.when(self.a >= d)
            def _():
                if receive:
                    self.recv(half, self.a - d, column)
                self.right(half, self.a - d, column, act)
                if half == 0:
                    act(self.copy(half, self.a - d, column, 2))

            @pl.when(self.a + d < self.line)
            def _():
                if receive:
                    self.recv(half, self.a + d, column)
                self.left(half, self.a + d, column, act)
                if half == 0:
                    act(self.copy(half, self.a + d, column, 2))

    def finish(self):
        for other in range(self.line):
            self.recv(0, other, 1 - self.b)
        wait = lambda c: c.wait_send()
        self.start(wait)
        for go in (self.right, self.left):
            go(1, self.a, 1 - self.b, wait)
        for d in range(1, self.line):
            self.step(d, wait, False)


def greet(count):
    barrier = pltpu.get_barrier_semaphore()
    me, core = lax.axis_index("ep"), lax.axis_index("tp")
    line = count // 2
    a, b = me // 2, me % 2

    def say(ids):
        pl.semaphore_signal(barrier, inc=1, device_id=ids, device_id_type=MESH)

    say({"tp": 1 - core})
    say({"ep": a * 2 + 1 - b})

    @pl.when(a < line - 1)
    def _():
        say({"ep": jnp.minimum(a + 1, line - 1) * 2 + b})

    @pl.when(a > 0)
    def _():
        say({"ep": jnp.maximum(a - 1, 0) * 2 + b})

    edges = jnp.where(a < line - 1, 1, 0) + jnp.where(a > 0, 1, 0)
    pl.semaphore_wait(barrier, 2 + edges)


def to_partner(src, dst, send_sem, recv_sem):
    return pltpu.make_async_remote_copy(
        src_ref=src,
        dst_ref=dst,
        send_sem=send_sem,
        recv_sem=recv_sem,
        device_id={"tp": 1 - lax.axis_index("tp")},
        device_id_type=MESH,
    )


def rms(values, norm_gain):
    values = values.astype(jnp.float32)
    scale = lax.rsqrt(jnp.mean(values * values, axis=1, keepdims=True) + 1e-06)
    return (values * scale * norm_gain).astype(jnp.bfloat16)


def front_kernel(
    count,
    query, key, value, weight, text_ref, gain, grid_ref,
    normed_out, visual_out, grid_out,
    kv, text, att, vis, grid, part, part_in,
    kv_send, kv_recv, text_send, text_recv, att_send, att_recv, vis_send, vis_recv,
    grid_send, grid_recv, pair_send, pair_recv,
):
    me, core = lax.axis_index("ep"), lax.axis_index("tp")
    line = count // 2
    kv_gather = TreeGather(lambda h, s: kv.at[h, s], count, kv_send, kv_recv)
    text_gather = TreeGather(lambda h, s: text.at[core, h, s], count, text_send, text_recv)
    att_gather = TreeGather(lambda h, s: att.at[h, s], count, att_send, att_recv)
    vis_gather = TreeGather(lambda h, s: vis.at[core, h, s], count, vis_send, vis_recv)
    grid_gather = TreeGather(lambda h, s: grid.at[h, s], count, grid_send, grid_recv)

    kv[0, me] = key[...]
    kv[1, me] = value[...]
    greet(count)
    kv_gather.start()
    width = text_ref.shape[1]
    mine = text_ref.shape[0] // 2
    own = rms(text_ref[pl.ds(pl.multiple_of(core * mine, mine), mine), :], gain[...])
    text[core, 0, me] = own[:, : width // 2]
    text[core, 1, me] = own[:, width // 2 :]
    grid[0, me] = grid_ref[0]
    grid[1, me] = grid_ref[1]
    kv_gather.cross()
    for d in range(1, line):
        kv_gather.step(d)
    text_gather.start()
    grid_gather.start()
    kv_gather.finish()

    patches, features = query.shape
    keys = kv[0].reshape(count * patches, features)
    values = kv[1].reshape(count * patches, features)
    parts = []
    for head in range(features // HEAD_DIM):
        lanes = slice(head * HEAD_DIM, (head + 1) * HEAD_DIM)
        scores = lax.dot_general(
            query[:, lanes], keys[:, lanes], (((1,), (1,)), ((), ())),
            preferred_element_type=jnp.float32,
        ) * (HEAD_DIM ** (-0.5))
        weights = jnp.exp(scores - jnp.max(scores, axis=1, keepdims=True))
        sums = jnp.sum(weights, axis=1, keepdims=True)
        mixed = jnp.dot(
            weights.astype(jnp.bfloat16), values[:, lanes], preferred_element_type=jnp.float32
        )
        parts.append((mixed / sums).astype(jnp.bfloat16))
    attended = jnp.concatenate(parts, axis=1)
    rows = patches // MERGE
    for p in range(MERGE):
        att[p // 2, me, p % 2] = attended[p * rows : (p + 1) * rows]
    att_gather.start()
    text_gather.cross()
    text_gather.step(1)
    late = [d for d in range(2, line)]
    for d in late[: len(late) // 2]:
        text_gather.step(d)
    att_gather.cross()
    for d in range(1, line):
        att_gather.step(d)
    for d in late[len(late) // 2 :]:
        text_gather.step(d)
    att_gather.finish()
    grid_gather.cross()
    for d in range(1, line):
        grid_gather.step(d)

    total = None
    for p in range(MERGE):
        left = att[p // 2, :, p % 2].reshape(count * rows, features)
        term = jnp.dot(left, weight[p], preferred_element_type=jnp.float32)
        total = term if total is None else total + term
    half_rows = count * rows // 2
    part[0] = total[:half_rows]
    part[1] = total[half_rows:]
    swap = to_partner(part.at[1 - core], part_in, pair_send.at[0], pair_recv.at[0])
    swap.start()
    swap.wait()
    summed = (part[core] + part_in[...]).astype(jnp.bfloat16)
    quarter = half_rows // 2
    vis[core, 0, me] = summed[:quarter]
    vis[core, 1, me] = summed[quarter:]
    vis_gather.start()
    text_gather.finish()
    swap_text = to_partner(text.at[core], text.at[core], pair_send.at[1], pair_recv.at[1])
    swap_text.start()
    vis_gather.cross()
    for d in range(1, line):
        vis_gather.step(d)
    swap_text.wait_send()
    to_partner(text.at[1 - core], text.at[1 - core], pair_send.at[1], pair_recv.at[1]).wait_recv()
    for s in range(count):
        for c in range(2):
            for h in range(2):
                normed_out[
                    s * 2 * mine + c * mine : s * 2 * mine + (c + 1) * mine,
                    h * width // 2 : (h + 1) * width // 2,
                ] = text[c, h, s]
    grid_gather.finish()
    for s in range(count):
        for h in range(2):
            grid_out[s, h] = grid[h, s]
    vis_gather.finish()
    swap_vis = to_partner(vis.at[core], vis.at[core], pair_send.at[2], pair_recv.at[2])
    swap_vis.start()
    swap_vis.wait_send()
    to_partner(vis.at[1 - core], vis.at[1 - core], pair_send.at[2], pair_recv.at[2]).wait_recv()
    columns = weight.shape[2]
    base = count * 2 * mine
    for c in range(2):
        for h in range(2):
            first = (c * 2 + h) * quarter
            for s in range(count):
                visual_out[first : first + quarter, s * columns : (s + 1) * columns] = vis[c, h, s]
            normed_out[base + first : base + first + quarter, :] = rms(
                visual_out[first : first + quarter, :], gain[...]
            )


def front(query_rows, key_rows, value_rows, merger_weight, text_rows, norm_gain, grid):
    count = lax.axis_size("ep")
    patches, features = query_rows.shape
    rows = patches // MERGE
    text_count, width = text_rows.shape
    columns = merger_weight.shape[2]
    quarter = count * rows // 4
    queries = query_rows.reshape(rows, MERGE, features).transpose(1, 0, 2).reshape(patches, features)
    bf16, f32 = jnp.bfloat16, jnp.float32
    sems = []
    for _ in range(5):
        sems += [pltpu.SemaphoreType.DMA((2, count, 3)), pltpu.SemaphoreType.DMA((2, count))]
    vmem = pl.BlockSpec(memory_space=pltpu.VMEM)
    return pl.pallas_call(
        functools.partial(front_kernel, count),
        name="front",
        out_shape=(
            jax.ShapeDtypeStruct((count * (text_count + rows), width), bf16),
            jax.ShapeDtypeStruct((count * rows, width), bf16),
            jax.ShapeDtypeStruct((count,) + grid.shape, f32),
        ),
        in_specs=[vmem] * 7,
        out_specs=(vmem,) * 3,
        scratch_shapes=[
            pltpu.VMEM((2, count, patches, features), bf16),
            pltpu.VMEM((2, 2, count, text_count // 2, width // 2), bf16),
            pltpu.VMEM((2, count, 2, rows, features), bf16),
            pltpu.VMEM((2, 2, count, quarter, columns), bf16),
            pltpu.VMEM((2, count) + grid.shape[1:], f32),
            pltpu.VMEM((2, 2 * quarter, columns), f32),
            pltpu.VMEM((2 * quarter, columns), f32),
        ]
        + sems
        + [pltpu.SemaphoreType.DMA((3,)), pltpu.SemaphoreType.DMA((3,))],
        compiler_params=pltpu.CompilerParams(
            collective_id=0, has_side_effects=True, vmem_limit_bytes=56 * MIB
        ),
    )(queries, key_rows, value_rows, merger_weight, text_rows, norm_gain.reshape(1, -1), grid)


def back_kernel(
    count,
    normed, gates, pick, gate_hbm, up_hbm, down_hbm,
    out_ref,
    pair_w, down, hidden, acc, pin, cross0, cross1, zin, fin,
    load_sem, down_sem, pair_send, pair_recv, y_send, y_recv, z_send, z_recv,
):
    core, me = lax.axis_index("tp"), lax.axis_index("ep")
    line = count // 2
    a, b = me // 2, me % 2
    experts, width, units = gate_hbm.shape
    total_rows = normed.shape[0]
    visual = pick.shape[1]
    texts = (total_rows - visual) // count
    slots = pick.shape[0] // count
    span = acc.shape[4]
    slot_total = pair_w.shape[0]
    step_rows = 384 if total_rows % 384 == 0 else total_rows

    def load(e, which):
        slot = e % slot_total
        source = (gate_hbm, up_hbm)[which]
        return pltpu.make_async_copy(
            source.at[e], pair_w.at[slot, :, pl.ds(which * units, units)], load_sem.at[slot, which]
        )

    def load_down(e):
        return pltpu.make_async_copy(
            down_hbm.at[e], down.at[pl.ds(e * units, units), :], down_sem.at[e]
        )

    for e in range(slot_total):
        load(e, 0).start()
        load(e, 1).start()
    for e in range(experts):
        load_down(e).start()
    greet(count)

    @pl.loop(0, experts)
    def _(e):
        load(e, 0).wait()
        load(e, 1).wait()
        for first in range(0, total_rows, step_rows):
            rows = slice(first, first + step_rows)
            both = jnp.dot(
                normed[rows, :], pair_w[e % slot_total], preferred_element_type=jnp.float32
            )
            value = both[:, :units]
            gated = value / (1.0 + jnp.exp(-value)) * both[:, units:] * gates[e, rows, :]
            hidden[rows, pl.ds(pl.multiple_of(e * units, 128), units)] = gated.astype(jnp.bfloat16)

        @pl.when(e + slot_total < experts)
        def _():
            load(e + slot_total, 0).start()
            load(e + slot_total, 1).start()

    for e in range(experts):
        load_down(e).wait()
    chunk = 512
    base = total_rows - visual

    def half_sums(side, half, add):
        for offset in range(0, span, chunk):
            start = pl.multiple_of(side * 2 * span + half * span + offset, chunk)
            weight = down[:, pl.ds(start, chunk)]
            lanes = slice(offset, offset + chunk)
            text = jnp.dot(hidden[:base, :], weight, preferred_element_type=jnp.float32)
            seen = jnp.dot(hidden[base:, :], weight, preferred_element_type=jnp.float32)
            placed = jnp.dot(
                pick[...], seen.astype(jnp.bfloat16), preferred_element_type=jnp.float32
            )
            for s in range(count):
                sums = jnp.concatenate(
                    [text[s * texts : (s + 1) * texts], placed[s * slots : (s + 1) * slots]]
                )
                if add:
                    sums = sums + pin[half, s % 2, s // 2, :, lanes].astype(jnp.float32)
                acc[half, s % 2, s // 2, :, lanes] = sums.astype(jnp.bfloat16)

    swaps = [
        to_partner(acc.at[h], pin.at[h], pair_send.at[h], pair_recv.at[h]) for h in range(2)
    ]
    for h in range(2):
        half_sums(1 - core, h, False)
        swaps[h].start()

    def remote(src, dst, send_sem, recv_sem, target):
        return pltpu.make_async_remote_copy(
            src_ref=src, dst_ref=dst, send_sem=send_sem, recv_sem=recv_sem,
            device_id={"ep": target}, device_id_type=MESH,
        )

    other = a * 2 + 1 - b
    swaps[0].wait()
    half_sums(core, 0, True)
    first_cross = remote(acc.at[0, 1 - b], cross0, y_send.at[0], y_recv.at[0], other)
    first_cross.start()
    swaps[1].wait()
    half_sums(core, 1, True)

    places = ((0, b), (1, b), (1, 1 - b))

    def hop(q, target, way):
        half, column = places[q]
        towards = jnp.clip(a + (1, -1)[way], 0, line - 1) * 2 + b
        return remote(
            acc.at[half, column, target], zin.at[q, target + 1 - way],
            z_send.at[q, target, way], z_recv.at[q, target, way], towards,
        )

    def take(q, target, way):
        half, column = places[q]
        hop(q, target, way).wait_recv()
        acc[half, column, target] = (
            acc[half, column, target].astype(jnp.float32)
            + zin[q, target + 1 - way].astype(jnp.float32)
        ).astype(jnp.bfloat16)

    def flow(q, i):
        right, left = line - 1 - i, i

        @pl.when(right > a)
        def _():
            @pl.when(a > 0)
            def _():
                take(q, right, 0)

            hop(q, right, 0).start()

        @pl.when(left < a)
        def _():
            @pl.when(a < line - 1)
            def _():
                take(q, left, 1)

            hop(q, left, 1).start()

    def land(q):
        @pl.when(a > 0)
        def _():
            take(q, a, 0)

        @pl.when(a < line - 1)
        def _():
            take(q, a, 1)

    for i in range(min(2, line - 1)):
        flow(2, i)
        flow(1, i)
    first_cross.wait()
    for t in range(line):
        acc[0, b, t] = (
            acc[0, b, t].astype(jnp.float32) + cross0[t].astype(jnp.float32)
        ).astype(jnp.bfloat16)
    flow(0, 0)
    for i in range(2, line - 1):
        flow(2, i)
        flow(1, i)
        flow(0, i - 1)
    land(2)
    last_cross = remote(acc.at[1, 1 - b, a], cross1, y_send.at[1], y_recv.at[1], other)
    last_cross.start()
    if line > 2:
        flow(0, line - 2)
    land(1)
    land(0)
    fin[core, 0] = acc[0, b, a]
    last_cross.wait()
    fin[core, 1] = (
        acc[1, b, a].astype(jnp.float32) + cross1[...].astype(jnp.float32)
    ).astype(jnp.bfloat16)
    to_partner(fin.at[core], fin.at[core], pair_send.at[2], pair_recv.at[2]).start()
    for q in range(3):
        for t in range(line):

            @pl.when(t > a)
            def _():
                hop(q, t, 0).wait_send()

            @pl.when(t < a)
            def _():
                hop(q, t, 1).wait_send()

    to_partner(fin.at[core], fin.at[core], pair_send.at[2], pair_recv.at[2]).wait_send()
    to_partner(fin.at[1 - core], fin.at[1 - core], pair_send.at[2], pair_recv.at[2]).wait_recv()
    for c in range(2):
        for h in range(2):
            out_ref[:, (c * 2 + h) * span : (c * 2 + h + 1) * span] = fin[c, h]


def back(normed, gates, pick, gate_weight, up_weight, down_weight):
    count = lax.axis_size("ep")
    line = count // 2
    experts, width, units = gate_weight.shape
    total_rows = normed.shape[0]
    owned = (total_rows - pick.shape[1] + pick.shape[0]) // count
    span = width // 4
    bf16 = jnp.bfloat16
    dma = pltpu.SemaphoreType.DMA
    vmem, hbm = pl.BlockSpec(memory_space=pltpu.VMEM), pl.BlockSpec(memory_space=pl.ANY)
    return pl.pallas_call(
        functools.partial(back_kernel, count),
        name="back",
        out_shape=jax.ShapeDtypeStruct((owned, width), bf16),
        in_specs=[vmem] * 3 + [hbm] * 3,
        out_specs=vmem,
        scratch_shapes=[
            pltpu.VMEM((min(2, experts), width, 2 * units), bf16),
            pltpu.VMEM((experts * units, width), bf16),
            pltpu.VMEM((total_rows, experts * units), bf16),
            pltpu.VMEM((2, 2, line, owned, span), bf16),
            pltpu.VMEM((2, 2, line, owned, span), bf16),
            pltpu.VMEM((line, owned, span), bf16),
            pltpu.VMEM((owned, span), bf16),
            pltpu.VMEM((3, line + 1, owned, span), bf16),
            pltpu.VMEM((2, 2, owned, span), bf16),
            dma((2, 2)), dma((experts,)), dma((3,)), dma((3,)), dma((2,)), dma((2,)),
            dma((3, line, 2)), dma((3, line, 2)),
        ],
        compiler_params=pltpu.CompilerParams(
            collective_id=1, has_side_effects=True, vmem_limit_bytes=62 * MIB
        ),
    )(normed, gates, pick, gate_weight, up_weight, down_weight)


def body(
    query_rows,
    key_rows,
    value_rows,
    merger_weight,
    visual_counts,
    text_rows,
    norm_gain,
    route_ids,
    route_gates,
    gate_weight,
    up_weight,
    down_weight,
):
    owners = lax.axis_size("ep")
    owner = lax.axis_index("ep")
    patch_count = query_rows.shape[0]
    text_count = text_rows.shape[0]
    row_count = route_ids.shape[0]
    slot_count = row_count - text_count
    local_experts = gate_weight.shape[0]
    expert_count = local_experts * owners
    width = text_rows.shape[1]

    offsets = jnp.cumsum(visual_counts) - visual_counts
    positions = jnp.arange(slot_count, dtype=jnp.int32)
    live = jnp.concatenate(
        [jnp.ones((text_count,), jnp.bool_), positions < visual_counts[owner]]
    )
    named = route_ids[:, :, None] == jnp.arange(expert_count, dtype=jnp.int32)
    grid = jnp.sum(jnp.where(named & live[:, None, None], route_gates[:, :, None], 0.0), axis=1)
    flat = jnp.pad(grid.T, ((0, 0), (0, -row_count % 128)))
    flat = flat.reshape(2, expert_count // 2, -1)
    normed, visual, grids = front(
        query_rows, key_rows, value_rows, merger_weight, text_rows, norm_gain, flat
    )
    grids = grids.reshape(owners, owners, local_experts, -1)
    grids = lax.dynamic_index_in_dim(grids, owner, 1, False)[:, :, :row_count]
    grids = grids.transpose(0, 2, 1)
    sources = offsets[:, None] + positions[None, :]
    filled = positions[None, :] < visual_counts[:, None]
    visual_total = owners * patch_count // MERGE
    pick = (
        filled[:, :, None]
        & (sources[:, :, None] == jnp.arange(visual_total, dtype=jnp.int32))
    )
    text_grid = grids[:, :text_count].reshape(-1, local_experts)
    visual_grid = jnp.einsum(
        "ojv,oje->ve", pick.astype(jnp.float32), grids[:, text_count:],
        precision=lax.Precision.HIGHEST,
    )
    all_grid = jnp.concatenate([text_grid, visual_grid], axis=0)

    combined = back(
        normed,
        all_grid.T[:, :, None],
        pick.reshape(owners * slot_count, visual_total).astype(jnp.bfloat16),
        gate_weight,
        up_weight,
        down_weight,
    )
    my_visual = jnp.dot(
        pick[owner].astype(jnp.bfloat16), visual, preferred_element_type=jnp.float32
    ).astype(jnp.bfloat16)
    rows = jnp.concatenate([text_rows, my_visual], axis=0)
    return (rows.astype(jnp.float32) + combined.astype(jnp.float32)).astype(jnp.bfloat16)


def solution(mesh):
    return jax.shard_map(
        body,
        mesh=mesh,
        in_specs=(
            P(("grp", "ep"), "tp"),
            P(("grp", "ep"), "tp"),
            P(("grp", "ep"), "tp"),
            P(None, "tp", "ep"),
            P("grp"),
            P(("grp", "ep"), None),
            P(),
            P(("grp", "ep"), None),
            P(("grp", "ep"), None),
            P("ep", None, "tp"),
            P("ep", None, "tp"),
            P("ep", "tp", None),
        ),
        out_specs=P(("grp", "ep"), None),
        check_vma=False,
    )
```
